32 devices in a mesh: sub: 8 (over z, y), loc: 4 (over x, core).
Axes of the slice: x: 2, y: 2, z: 4, core: 2. Of those that a mesh axis runs over, the one named last changes fastest.
Arguments:
- load_cases: float32 [32, 256, 1024], P(('sub', 'loc')), may hold values from -6 to 6
- schur_matrix: bfloat16 [32, 1024, 1024], P(('sub', 'loc')), as said below
- neumann: bfloat16 [32, 1024, 1024], P(('sub', 'loc')), as said below
- stiffness: float32 [32, 1024], P(('sub', 'loc')), may hold values from 0.1 to 10
- face_map: int32 [32, 2, 256], P(('sub', 'loc')), may hold values from 0 to 255, each once within a row
- coarse_basis: float32 [32, 1024, 16], P(('sub', 'loc')), may hold values from -0.5 to 0.5
- corner_map: int32 [32, 16], P(('sub', 'loc')), may hold values from 0 to 31, as said below
- owner_map: int32 [8, 32], P('sub'), may hold values from 0 to 3, as said below
- level2_inverse: float32 [8, 32, 32], P('sub'), as said below
- level3_map: int32 [8, 32], P('sub'), may hold values from 0 to 63, as said below
- level3_weight: float32 [8, 32], P('sub'), may hold values from 0.5 to 1.5
- level3_inverse: float32 [64, 64], replicated, as said below
Outputs:
- solution: float32 [32, 256, 1024], P(('sub', 'loc'))
- residual: float32 [32, 256, 1024], P(('sub', 'loc'))
The draws below stay inside these ranges and needn't reach their ends.
Inputs may be any that keep to these rules, and one draw needn't show every extreme that they name: Each face_map[g, i] is a permutation. `corner_map`: within each group every level-2 degree of freedom is named by some entry of its 4 subdomains. `owner_map`: within one group at most 16 level-2 degrees of freedom have the same owner, and some owner has exactly 16. `level3_map`: every level-3 degree of freedom is named. `schur_matrix`: each matrix is symmetric positive definite. `neumann`: each matrix is symmetric positive definite. `level2_inverse`: each matrix is symmetric positive definite. `level3_inverse`: symmetric positive definite.
All inputs are finite; a program needn't handle non-finite values.
Results may differ from the reference program's by a relative error of at most 0.0031.
Values sent between devices are 32-bit elements; how exact they have to be, the bound alone decides.
A program may use at most 64 MiB of HBM per device.

```python
import math
import jax
import jax.numpy as jnp
from jax import lax

NI = 1024
FACE = 256
LOADS = 256
NCL = 16
ITERS = 2
GROUPS = 8
GROUP_SIZE = 4
SUBDOMAINS = 32
NC2 = 32
NC3 = 64


off_ratio = 0.6


def spd_draw(key, matrices, order, low, high):
    key_noise, key_diag = jax.random.split(key)
    noise_draw = jax.random.uniform(key_noise, (matrices, order, order), jnp.float32, -1.0, 1.0)
    symmetric = 0.5 * (noise_draw + jnp.swapaxes(noise_draw, 1, 2))
    entry_scale = off_ratio * low * math.sqrt(6.0) / (2.0 * math.sqrt(order))
    diagonal = jax.random.uniform(key_diag, (matrices, order), jnp.float32, low, high)
    return symmetric * entry_scale + diagonal[:, :, None] * jnp.eye(order, dtype=jnp.float32)


def draw_schur_matrix(key, part):
    key = jax.random.fold_in(key, 5)
    return spd_draw(key, SUBDOMAINS, NI, 1.2, 1.9).astype(jnp.bfloat16)


def draw_neumann(key, part):
    key = jax.random.fold_in(key, 7)
    return spd_draw(key, SUBDOMAINS, NI, 0.4, 0.64).astype(jnp.bfloat16)


def draw_level2_inverse(key, part):
    key = jax.random.fold_in(key, 9)
    return spd_draw(key, GROUPS, NC2, 0.6, 0.95)


def draw_level3_inverse(key, part):
    key = jax.random.fold_in(key, 13)
    return spd_draw(key, 1, NC3, 0.6, 0.95)[0]


def draw_corner_map(key, part):
    key = jax.random.fold_in(key, 21)
    group_count = SUBDOMAINS * NCL // (2 * NC2)

    def one_group(group_key):
        key_fill, key_order = jax.random.split(group_key)
        values = jnp.concatenate([jnp.arange(NC2, dtype=jnp.int32), jax.random.randint(key_fill, (NC2,), 0, NC2, dtype=jnp.int32)])
        return jax.random.permutation(key_order, values)
    return jax.vmap(one_group)(jax.random.split(key, group_count)).reshape(SUBDOMAINS, NCL)


def draw_owner_map(key, part):
    key = jax.random.fold_in(key, 31)
    owner_count = 2 * NC2 // NCL

    def one_group(group_key):
        key_first, key_offset, key_order = jax.random.split(group_key, 3)
        first_owner = jax.random.randint(key_first, (), 0, owner_count, dtype=jnp.int32)
        offset = jax.random.randint(key_offset, (), 0, owner_count - 1, dtype=jnp.int32)
        position = jnp.arange(NC2, dtype=jnp.int32)
        other_owner = (first_owner + 1 + (position + offset) % (owner_count - 1)) % owner_count
        owner_raw = jnp.where(position < NCL, first_owner, other_owner)
        return jax.random.permutation(key_order, owner_raw)
    return jax.vmap(one_group)(jax.random.split(key, GROUPS))


def draw_level3_map(key, part):
    key = jax.random.fold_in(key, 41)
    key_fill, key_order = jax.random.split(key)
    dof_count = GROUPS * NC2
    values = jnp.concatenate([jnp.arange(NC3, dtype=jnp.int32), jax.random.randint(key_fill, (dof_count - NC3,), 0, NC3, dtype=jnp.int32)])
    return jax.random.permutation(key_order, values).reshape(GROUPS, NC2)


def level_of(key, extent, cuts, least, top_value):
    factor_of, own = 1.0, jax.random.fold_in(key, 6)
    for dim, shards_of in cuts:
        draws = jnp.exp(jax.random.uniform(jax.random.fold_in(own, dim), (shards_of,), jnp.float32, least / len(cuts), top_value / len(cuts)))
        factor_of = factor_of * jnp.repeat(draws, extent[dim] // shards_of).reshape([-1 if axis == dim else 1 for axis in range(len(extent))])
    return factor_of


def bell_draw(stream_key, dims, spread, bound, pieces=(), kind=jnp.bfloat16):
    array = jax.random.normal(stream_key, dims, jnp.float32) * spread
    if len(pieces) > 0:
        array = level_of(stream_key, dims, pieces, -0.22, 0.18) * array
    return jnp.clip(array, min=-bound, max=bound).astype(kind)


def setup_inputs(seed: int = 0) -> dict:
    keys = jax.random.split(jax.random.key(seed), 13)
    return {
        "load_cases": bell_draw(keys[0], (SUBDOMAINS, LOADS, NI), 1.0, 6.0, ((0, 32),), jnp.float32),
        "schur_matrix": draw_schur_matrix(jax.random.fold_in(keys[12], 71), 0),
        "neumann": draw_neumann(jax.random.fold_in(keys[12], 71), 0),
        "stiffness": jnp.clip(jnp.exp(math.log(10.0) - 4.6051702 * jax.random.uniform(keys[3], (SUBDOMAINS, NI), jnp.float32) ** level_of(keys[3], (SUBDOMAINS, NI), ((0, 32),), -0.2, 0.2)), 0.1, 10.0),
        "face_map": jax.vmap(lambda own: jax.random.permutation(own, FACE))(jax.random.split(keys[4], SUBDOMAINS * 2)).reshape((SUBDOMAINS, 2, FACE)).astype(jnp.int32),
        "coarse_basis": bell_draw(keys[5], (SUBDOMAINS, NI, NCL), 0.0625, 0.5, ((0, 32),), jnp.float32),
        "corner_map": draw_corner_map(jax.random.fold_in(keys[12], 71), 0),
        "owner_map": draw_owner_map(jax.random.fold_in(keys[12], 71), 0),
        "level2_inverse": draw_level2_inverse(jax.random.fold_in(keys[12], 71), 0),
        "level3_map": draw_level3_map(jax.random.fold_in(keys[12], 71), 0),
        "level3_weight": jnp.clip(0.5 + 1.0 * jax.random.uniform(keys[10], (GROUPS, NC2), jnp.float32) ** level_of(keys[10], (GROUPS, NC2), ((0, 8),), -0.2, 0.2), 0.5, 1.5),
        "level3_inverse": draw_level3_inverse(jax.random.fold_in(keys[12], 71), 0),
    }


highest = lax.Precision.HIGHEST


def face_permute(face_values, order_index):
    return jax.vmap(jax.vmap(lambda row_values, row_order: jnp.take(row_values, row_order, axis=-1)))(face_values, order_index)


def shared_sum(values, face_map):
    layout = values.reshape((GROUPS, GROUP_SIZE) + values.shape[1:])
    face_maps = face_map.reshape(GROUPS, GROUP_SIZE, 2, FACE)
    left_map = face_maps[:, :, 0]
    top_map = face_maps[:, :, 1]
    left_back = jnp.argsort(left_map, axis=-1).astype(jnp.int32)
    top_back = jnp.argsort(top_map, axis=-1).astype(jnp.int32)
    left_face = layout[..., :FACE]
    right_face = layout[..., FACE:2 * FACE]
    top_face = layout[..., 2 * FACE:3 * FACE]
    bottom_face = layout[..., 3 * FACE:]
    zero_sub = jnp.zeros_like(left_face[:1])
    zero_loc = jnp.zeros_like(left_face[:, :1])
    from_left = jnp.concatenate([zero_sub, right_face[:-1]], axis=0)
    to_left = face_permute(left_face, left_back)
    from_right = jnp.concatenate([to_left[1:], zero_sub], axis=0)
    from_above = jnp.concatenate([zero_loc, bottom_face[:, :-1]], axis=1)
    to_above = face_permute(top_face, top_back)
    from_below = jnp.concatenate([to_above[:, 1:], zero_loc], axis=1)
    joined = jnp.concatenate([left_face + face_permute(from_left, left_map), right_face + from_right,
                              top_face + face_permute(from_above, top_map), bottom_face + from_below], axis=-1)
    return joined.reshape(values.shape)


def precondition(resid_field, weights, neumann, coarse_basis, corner_map, owner_map, level2_inverse,
                 level3_map, level3_weight, level3_inverse, face_map):
    restricted = weights * resid_field
    rounded = restricted.astype(jnp.bfloat16)
    local_solve = lax.map(lambda operands: jnp.dot(operands[0], operands[1], preferred_element_type=jnp.float32),
                          (rounded, neumann))
    coarse = jnp.einsum('sln,snc->scl', restricted, coarse_basis, precision=highest)
    corner_onehot = (corner_map[:, None, :] == jnp.arange(NC2, dtype=jnp.int32)[None, :, None]).astype(jnp.float32)
    per_subdomain = jnp.einsum('skc,scl->skl', corner_onehot, coarse, precision=highest)
    level2 = jnp.sum(per_subdomain.reshape(GROUPS, GROUP_SIZE, NC2, LOADS), axis=1)
    same_owner = (owner_map[:, :, None] == owner_map[:, None, :]).astype(jnp.float32)
    owner_update = jnp.einsum('gkm,gml->gkl', level2_inverse * same_owner, level2, precision=highest)
    level3_onehot = (level3_map[:, None, :] == jnp.arange(NC3, dtype=jnp.int32)[None, :, None]).astype(jnp.float32)
    weighted = level3_weight[:, :, None] * level2
    level3 = jnp.einsum('gmk,gkl->ml', level3_onehot, weighted, precision=highest)
    level3_update = jnp.dot(level3_inverse, level3, precision=highest)
    back_level3 = jnp.einsum('gmk,ml->gkl', level3_onehot, level3_update, precision=highest) * level3_weight[:, :, None]
    level2_update = owner_update + back_level3
    spread_update = jnp.broadcast_to(level2_update[:, None], (GROUPS, GROUP_SIZE, NC2, LOADS)).reshape(SUBDOMAINS, NC2, LOADS)
    corner_update = jnp.einsum('skc,skl->scl', corner_onehot, spread_update, precision=highest)
    fine_update = local_solve + jnp.einsum('snc,scl->sln', coarse_basis, corner_update, precision=highest)
    return shared_sum(weights * fine_update, face_map)


def reference(load_cases, schur_matrix, neumann, stiffness, face_map, coarse_basis, corner_map, owner_map,
              level2_inverse, level3_map, level3_weight, level3_inverse):
    right_side = shared_sum(load_cases, face_map)
    weights = (stiffness / shared_sum(stiffness, face_map))[:, None, :]

    def inner(first_field, second_field):
        return jnp.sum(weights * first_field * second_field)

    def apply_precond(resid_field):
        return precondition(resid_field, weights, neumann, coarse_basis, corner_map, owner_map, level2_inverse,
                            level3_map, level3_weight, level3_inverse, face_map)

    solution = jnp.zeros_like(right_side)
    residual = right_side
    precond = apply_precond(residual)
    direction = precond
    current = inner(residual, precond)
    for iteration in range(ITERS):
        rounded = direction.astype(jnp.bfloat16)
        product = lax.map(lambda operands: jnp.dot(operands[0], operands[1], preferred_element_type=jnp.float32),
                          (rounded, schur_matrix))
        image_field = shared_sum(product, face_map)
        step_size = current / inner(direction, image_field)
        solution = solution + step_size * direction
        residual = residual - step_size * image_field
        if iteration + 1 < ITERS:
            precond = apply_precond(residual)
            following = inner(residual, precond)
            direction = precond + (following / current) * direction
            current = following
    return solution, residual
```

```python
import functools

import jax
import jax.numpy as jnp
from jax import lax
from jax.experimental import pallas as pl
from jax.experimental.pallas import tpu as pltpu
from jax.sharding import PartitionSpec as P

ITERS = 2
EXCHANGES = 1 + 2 * ITERS
MESH = pl.DeviceIdType.MESH
highest = lax.Precision.HIGHEST
f32 = jnp.float32
bf16 = jnp.bfloat16


def dot(a, b, contract=(1, 0), precision=None):
    return lax.dot_general(
        a,
        b,
        (((contract[0],), (contract[1],)), ((), ())),
        precision=precision,
        preferred_element_type=f32,
    )


def tile_sum(block):
    rows, cols = block.shape
    folded = jnp.sum(block.reshape(rows // 8, 8, cols), axis=0)
    total = folded[:, :128]
    for start in range(128, cols, 128):
        total = total + folded[:, start : start + 128]
    return total


def kernel(
    subs,
    locs,
    load_hbm,
    schur_hbm,
    neumann_hbm,
    stiff,
    face_map,
    basis,
    corner,
    owner,
    inverse_two,
    level3_map,
    level3_weight,
    inverse_three,
    solution_out,
    residual_out,
    base,
    received0,
    received,
    schur,
    neumann,
    schur_raw,
    neumann_raw,
    turn,
    weight,
    group_basis,
    level3_scatter,
    r,
    fields,
    rounded,
    direction,
    direction2,
    level2_parts,
    level3_parts,
    level3_rows,
    scalar_loc,
    scalar_sub,
    load_sem,
    face_send,
    face_recv,
    l2_send,
    l2_recv,
    l3_send,
    l3_recv,
    rows_send,
    rows_recv,
    sl_send,
    sl_recv,
    ss_send,
    ss_recv,
):
    me_sub, me_loc = lax.axis_index("sub"), lax.axis_index("loc")
    loads = load_hbm.shape[0]
    width = face_map.shape[-1]
    level2_count = inverse_two.shape[-1]
    level3_count = inverse_three.shape[-1]
    cols = [slice(f * width, (f + 1) * width) for f in range(4)]

    load_copies = [
        pltpu.make_async_copy(load_hbm, base.at[pl.ds(0, loads)], load_sem.at[0]),
        pltpu.make_async_copy(neumann_hbm, neumann_raw, load_sem.at[1]),
        pltpu.make_async_copy(schur_hbm, schur_raw, load_sem.at[2]),
    ]
    for copy in load_copies:
        copy.start()

    barrier = pltpu.get_barrier_semaphore()
    for axis, count, me in (("sub", subs, me_sub), ("loc", locs, me_loc)):
        for d in range(1, count):
            pl.semaphore_signal(
                barrier,
                inc=1,
                device_id={axis: lax.rem(me + d, count)},
                device_id_type=MESH,
            )

    present = (me_sub > 0, me_sub < subs - 1, me_loc > 0, me_loc < locs - 1)
    partner = (
        {"sub": jnp.maximum(me_sub - 1, 0)},
        {"sub": jnp.minimum(me_sub + 1, subs - 1)},
        {"loc": jnp.maximum(me_loc - 1, 0)},
        {"loc": jnp.minimum(me_loc + 1, locs - 1)},
    )
    pending = []

    def face_copy(field, slots, e, f, slot):
        return pltpu.make_async_remote_copy(
            src_ref=field.at[:, cols[f]],
            dst_ref=slots.at[slot],
            send_sem=face_send.at[e, f],
            recv_sem=face_recv.at[e, slot],
            device_id=partner[f],
            device_id_type=MESH,
        )

    def send_face(field, slots, e, f):
        @pl.when(present[f])
        def _():
            face_copy(field, slots, e, f, f ^ 1).start()

        def finish():
            @pl.when(present[f])
            def _():
                face_copy(field, slots, e, f, f ^ 1).wait_send()

        pending.append(finish)

    def receive_face(field, slots, e, f, then):
        @pl.when(present[f])
        def _():
            face_copy(field, slots, e, f, f).wait_recv()
            then()

    def spread(axis, slots, send_sem, recv_sem):
        count, me = (subs, me_sub) if axis == "sub" else (locs, me_loc)

        def make(d, slot):
            peer = lax.rem(me + d, count)
            slot = me if slot is None else peer
            return pltpu.make_async_remote_copy(
                src_ref=slots.at[me],
                dst_ref=slots.at[slot],
                send_sem=send_sem.at[d - 1],
                recv_sem=recv_sem.at[slot],
                device_id={axis: peer},
                device_id_type=MESH,
            )

        for d in range(1, count):
            make(d, None).start()

        def finish():
            for d in range(1, count):
                make(d, None).wait_send()

        pending.append(finish)

        def wait():
            for d in range(1, count):
                make(d, "peer").wait_recv()

        return wait

    def total_of(slots, count):
        total = slots[0]
        for i in range(1, count):
            total = total + slots[i]
        return total

    rows_iota = lax.broadcasted_iota(jnp.int32, (width, width), 0)
    for i in range(2):
        turn[i] = (face_map[i : i + 1, :] == rows_iota).astype(f32)

    load_copies[0].wait()
    base[loads : loads + 8, :] = jnp.broadcast_to(stiff[...], (8, stiff.shape[-1]))
    pl.semaphore_wait(barrier, subs + locs - 2)
    for f in (1, 3):
        send_face(base, received0, 0, f)
    for f in (0, 2):
        base[:, cols[f]] = dot(base[:, cols[f]], turn[f // 2], (1, 1), highest)
        send_face(base, received0, 0, f)

    def reorder(source, target):
        for f in (0, 2):
            one_hot = turn[f // 2].astype(bf16)
            source[cols[f], :] = dot(one_hot, source[cols[f], :]).astype(bf16)
        for f in (0, 2):
            one_hot = turn[f // 2].astype(bf16)
            target[:, cols[f]] = dot(source[:, cols[f]], one_hot, (1, 1)).astype(bf16)
        for f in (1, 3):
            target[:, cols[f]] = source[:, cols[f]]

    load_copies[1].wait()
    reorder(neumann_raw, neumann)
    load_copies[2].wait()
    reorder(schur_raw, schur)

    def named(row, count):
        shape = (count, row.shape[-1])
        return (row == lax.broadcasted_iota(jnp.int32, shape, 0)).astype(f32)

    corner_hot = named(corner[...], level2_count)
    for f in range(4):
        part = dot(corner_hot, basis[cols[f], :], (1, 1), highest)
        if f in (0, 2):
            part = dot(part, turn[f // 2], (1, 1), highest)
        group_basis[:, cols[f]] = part
    level3_scatter[...] = named(level3_map[...], level3_count) * level3_weight[...]
    owner_hot = named(owner[...], max(8, locs))
    masked_two = inverse_two[...] * dot(owner_hot, owner_hot, (0, 0))
    back_three = dot(level3_scatter[...], inverse_three[...], (0, 0), highest)

    for f in (2, 3, 0, 1):
        r[:, cols[f]] = base[:loads, cols[f]]
        weight[:, cols[f]] = base[loads:, cols[f]]

        def add(f=f):
            r[:, cols[f]] += received0[f, :loads]
            weight[:, cols[f]] += received0[f, loads:]

        receive_face(base, received0, 0, f, add)
        weight[:, cols[f]] = base[loads:, cols[f]] / weight[:, cols[f]]
    for f in range(4):
        group_basis[:, cols[f]] *= weight[0:1, cols[f]]

    class Total:
        def __init__(self, i, tile):
            self.i = i
            scalar_loc[i, me_loc] = tile
            self.wait = spread("loc", scalar_loc.at[i], sl_send.at[i], sl_recv.at[i])

        def cross(self):
            self.wait()
            i = self.i
            scalar_sub[i, me_sub] = total_of(scalar_loc.at[i], locs)
            self.wait = spread("sub", scalar_sub.at[i], ss_send.at[i], ss_recv.at[i])

        def value(self):
            self.wait()
            return jnp.sum(total_of(scalar_sub.at[self.i], subs))

    def precondition(k, e):
        z = fields.at[e - 1]
        level2 = jnp.zeros((level2_count, loads), f32)
        for f in range(4):
            rounded[:, cols[f]] = (weight[0:1, cols[f]] * r[:, cols[f]]).astype(bf16)
            level2 += dot(group_basis[:, cols[f]], r[:, cols[f]], (1, 1), highest)
        level2_parts[k, me_loc] = level2
        wait = spread("loc", level2_parts.at[k], l2_send.at[k], l2_recv.at[k])
        for f in (0, 1):
            z[:, cols[f]] = dot(rounded[...], neumann[:, cols[f]]) * weight[0:1, cols[f]]
        wait()
        level2 = total_of(level2_parts.at[k], locs)
        share = level3_count // locs
        mine = level3_scatter[pl.ds(pl.multiple_of(me_loc * share, 8), share), :]
        level3_parts[k, me_sub] = dot(mine, level2, precision=highest)
        wait = spread("sub", level3_parts.at[k], l3_send.at[k], l3_recv.at[k])
        for f in (2, 3):
            z[:, cols[f]] = dot(rounded[...], neumann[:, cols[f]]) * weight[0:1, cols[f]]
        owned = dot(masked_two, level2, precision=highest)
        wait()
        level3_rows[k, me_loc] = total_of(level3_parts.at[k], subs)
        wait = spread("loc", level3_rows.at[k], rows_send.at[k], rows_recv.at[k])
        wait()
        level3 = level3_rows[k].reshape(level3_count, loads)
        update = owned + dot(back_three, level3, precision=highest)
        tile = jnp.zeros((8, 128), f32)
        for f in (0, 1, 2, 3):
            z[:, cols[f]] += dot(update, group_basis[:, cols[f]], (0, 0), highest)
            send_face(z, received.at[e - 1], e, f)
            tile += tile_sum(z[:, cols[f]] * r[:, cols[f]])
        return Total(2 * k, tile)

    def multiply(k, e, source):
        image = fields.at[e - 1]
        for f in range(4):
            rounded[:, cols[f]] = source[:, cols[f]].astype(bf16)
        tile = jnp.zeros((8, 128), f32)
        for f in (0, 1, 2, 3):
            image[:, cols[f]] = dot(rounded[...], schur[:, cols[f]])
            send_face(image, received.at[e - 1], e, f)
            tile += tile_sum(image[:, cols[f]] * source[:, cols[f]])
        return Total(2 * k + 1, tile)

    order = (2, 3, 0, 1)
    previous = None
    current = None
    out_direction = None
    for k in range(ITERS):
        e = 1 + 2 * k
        going = precondition(k, e)
        going.cross()
        z = fields.at[e - 1]
        target = direction if k == 0 else direction2
        for f in order:
            target[:, cols[f]] = z[:, cols[f]]

            def add(f=f):
                target[:, cols[f]] += received[e - 1, f]

            receive_face(z, received.at[e - 1], e, f, add)
        following = going.value()
        if k > 0:
            ratio = following / current
            for f in order:
                target[:, cols[f]] += ratio * direction[:, cols[f]]
        current = following
        e = e + 1
        image = fields.at[e - 1]
        going = multiply(k, e, target)
        going.cross()
        step = current / going.value()
        last = k + 1 == ITERS
        for f in order:
            r[:, cols[f]] -= step * image[:, cols[f]]

            def subtract(f=f):
                r[:, cols[f]] -= step * received[e - 1, f]

            receive_face(image, received.at[e - 1], e, f, subtract)
            if k == 0:
                solution_out[:, cols[f]] = step * target[:, cols[f]]
            else:
                solution_out[:, cols[f]] += step * target[:, cols[f]]
            if last and f in (0, 2):
                one_hot = turn[f // 2]
                solution_out[:, cols[f]] = dot(
                    solution_out[:, cols[f]], one_hot, precision=highest
                )
                residual_out[:, cols[f]] = dot(r[:, cols[f]], one_hot, precision=highest)
            elif last:
                residual_out[:, cols[f]] = r[:, cols[f]]

    for finish in pending:
        finish()


def on_device(mesh, *operands):
    subs, locs = mesh.shape["sub"], mesh.shape["loc"]
    (
        load_cases,
        schur_matrix,
        neumann,
        stiffness,
        face_map,
        basis,
        corner_map,
        owner_map,
        level2_inverse,
        level3_map,
        level3_weight,
        level3_inverse,
    ) = operands
    loads, order = load_cases.shape[1:]
    width = face_map.shape[-1]
    level2_count = level2_inverse.shape[-1]
    level3_count = level3_inverse.shape[-1]
    share = level3_count // locs
    vmem = pl.BlockSpec(memory_space=pltpu.VMEM)
    hbm = pl.BlockSpec(memory_space=pl.ANY)
    dma = pltpu.SemaphoreType.DMA
    field = jax.ShapeDtypeStruct((loads, order), f32)
    extra = EXCHANGES - 1
    totals = 2 * ITERS
    scratch = [
        pltpu.VMEM((loads + 8, order), f32),
        pltpu.VMEM((4, loads + 8, width), f32),
        pltpu.VMEM((extra, 4, loads, width), f32),
        pltpu.VMEM((order, order), bf16),
        pltpu.VMEM((order, order), bf16),
        pltpu.VMEM((order, order), bf16),
        pltpu.VMEM((order, order), bf16),
        pltpu.VMEM((2, width, width), f32),
        pltpu.VMEM((8, order), f32),
        pltpu.VMEM((level2_count, order), f32),
        pltpu.VMEM((level3_count, level2_count), f32),
        pltpu.VMEM((loads, order), f32),
        pltpu.VMEM((extra, loads, order), f32),
        pltpu.VMEM((loads, order), bf16),
        pltpu.VMEM((loads, order), f32),
        pltpu.VMEM((loads, order), f32),
        pltpu.VMEM((ITERS, locs, level2_count, loads), f32),
        pltpu.VMEM((ITERS, subs, share, loads), f32),
        pltpu.VMEM((ITERS, locs, share, loads), f32),
        pltpu.VMEM((totals, locs, 8, 128), f32),
        pltpu.VMEM((totals, subs, 8, 128), f32),
        dma((3,)),
        dma((EXCHANGES, 4)),
        dma((EXCHANGES, 4)),
        dma((ITERS, locs)),
        dma((ITERS, locs)),
        dma((ITERS, subs)),
        dma((ITERS, subs)),
        dma((ITERS, locs)),
        dma((ITERS, locs)),
        dma((totals, locs)),
        dma((totals, locs)),
        dma((totals, subs)),
        dma((totals, subs)),
    ]
    outputs = pl.pallas_call(
        functools.partial(kernel, subs, locs),
        out_shape=(field, field),
        in_specs=[hbm] * 3 + [vmem] * 9,
        out_specs=(vmem, vmem),
        scratch_shapes=scratch,
        compiler_params=pltpu.CompilerParams(
            collective_id=0, has_side_effects=True, vmem_limit_bytes=56 * 1024 * 1024
        ),
    )(
        load_cases[0],
        schur_matrix[0],
        neumann[0],
        stiffness,
        face_map[0],
        basis[0],
        corner_map,
        owner_map,
        level2_inverse[0],
        level3_map,
        level3_weight,
        level3_inverse,
    )
    return tuple(value[None] for value in outputs)


def solution(mesh):
    both = ("sub", "loc")
    cube, flat = P(both, None, None), P(both, None)
    group, group_cube = P("sub", None), P("sub", None, None)
    placed = (cube, cube, cube, flat, cube, cube, flat, group, group_cube, group, group, P())
    return jax.shard_map(
        functools.partial(on_device, mesh),
        mesh=mesh,
        in_specs=placed,
        out_specs=(cube, cube),
        check_vma=False,
    )
```

```python
import functools

import jax
import jax.numpy as jnp
from jax import lax
from jax.experimental import pallas as pl
from jax.experimental.pallas import tpu as pltpu
from jax.sharding import PartitionSpec as P

ITERS = 2
EXCHANGES = 1 + 2 * ITERS
CHUNKS = 2
MESH = pl.DeviceIdType.MESH
highest = lax.Precision.HIGHEST
f32 = jnp.float32
bf16 = jnp.bfloat16


def dot(a, b, contract=(1, 0), precision=None):
    return lax.dot_general(
        a,
        b,
        (((contract[0],), (contract[1],)), ((), ())),
        precision=precision,
        preferred_element_type=f32,
    )


def tile_sum(block):
    rows, cols = block.shape
    folded = jnp.sum(block.reshape(rows // 8, 8, cols), axis=0)
    total = folded[:, :128]
    for start in range(128, cols, 128):
        total = total + folded[:, start : start + 128]
    return total


def kernel(
    subs,
    locs,
    load_hbm,
    schur_hbm,
    neumann_hbm,
    stiff,
    face_map,
    basis,
    corner,
    owner,
    inverse_two,
    level3_map,
    level3_weight,
    inverse_three,
    solution_out,
    residual_out,
    base,
    received0,
    received,
    schur,
    neumann,
    schur_raw,
    neumann_raw,
    turn,
    weight,
    group_basis,
    weighted_basis,
    joint_basis,
    basis_in,
    level3_scatter,
    scatter_in,
    owned_mine,
    owned_in,
    r,
    fields,
    rounded,
    direction,
    direction2,
    solved,
    level2_parts,
    level3_parts,
    level3_rows,
    scalar_loc,
    scalar_sub,
    load_sem,
    out_sem,
    face_send,
    face_recv,
    basis_send,
    basis_recv,
    scatter_send,
    scatter_recv,
    owned_send,
    owned_recv,
    l2_send,
    l2_recv,
    l3_send,
    l3_recv,
    rows_send,
    rows_recv,
    sl_send,
    sl_recv,
    ss_send,
    ss_recv,
):
    me_sub, me_loc = lax.axis_index("sub"), lax.axis_index("loc")
    loads = load_hbm.shape[0]
    width = face_map.shape[-1]
    level2_count = inverse_two.shape[-1]
    level3_count = inverse_three.shape[-1]
    cols = [slice(f * width, (f + 1) * width) for f in range(4)]
    chunk = loads // CHUNKS
    rows = [slice(c * chunk, (c + 1) * chunk) for c in range(CHUNKS)]
    order = (2, 3, 0, 1)

    load_copies = [
        pltpu.make_async_copy(load_hbm, base.at[pl.ds(8, loads)], load_sem.at[0]),
        pltpu.make_async_copy(neumann_hbm, neumann_raw, load_sem.at[1]),
        pltpu.make_async_copy(schur_hbm, schur_raw, load_sem.at[2]),
    ]
    for copy in load_copies:
        copy.start()

    barrier = pltpu.get_barrier_semaphore()
    for axis, count, me in (("sub", subs, me_sub), ("loc", locs, me_loc)):
        for d in range(1, count):
            pl.semaphore_signal(
                barrier,
                inc=1,
                device_id={axis: lax.rem(me + d, count)},
                device_id_type=MESH,
            )

    present = (me_sub > 0, me_sub < subs - 1, me_loc > 0, me_loc < locs - 1)
    partner = (
        {"sub": jnp.maximum(me_sub - 1, 0)},
        {"sub": jnp.minimum(me_sub + 1, subs - 1)},
        {"loc": jnp.maximum(me_loc - 1, 0)},
        {"loc": jnp.minimum(me_loc + 1, locs - 1)},
    )
    pending = []

    class Neighbour:
        def __init__(self, f, source, slot, send_sem, recv_sem):
            self.f = f
            self.make = lambda at: pltpu.make_async_remote_copy(
                src_ref=source,
                dst_ref=slot(at),
                send_sem=send_sem.at[f],
                recv_sem=recv_sem.at[at],
                device_id=partner[f],
                device_id_type=MESH,
            )

        def send(self):
            @pl.when(present[self.f])
            def _():
                self.make(self.f ^ 1).start()

            def finish():
                @pl.when(present[self.f])
                def _():
                    self.make(self.f ^ 1).wait_send()

            pending.append(finish)

        def receive(self, then):
            @pl.when(present[self.f])
            def _():
                self.make(self.f).wait_recv()
                then()

    def face(field, slots, e, c, f, part):
        return Neighbour(
            f,
            field.at[part, cols[f]],
            lambda at: slots.at[at, part],
            face_send.at[e, c],
            face_recv.at[e, c],
        )

    def spread(axis, slots, send_sem, recv_sem):
        count, me = (subs, me_sub) if axis == "sub" else (locs, me_loc)

        def make(d, slot):
            peer = lax.rem(me + d, count)
            slot = me if slot is None else peer
            return pltpu.make_async_remote_copy(
                src_ref=slots.at[me],
                dst_ref=slots.at[slot],
                send_sem=send_sem.at[d - 1],
                recv_sem=recv_sem.at[slot],
                device_id={axis: peer},
                device_id_type=MESH,
            )

        for d in range(1, count):
            make(d, None).start()

        def finish():
            for d in range(1, count):
                make(d, None).wait_send()

        pending.append(finish)

        def wait():
            for d in range(1, count):
                make(d, "peer").wait_recv()

        return wait

    def total_of(slots, count):
        total = slots[0]
        for i in range(1, count):
            total = total + slots[i]
        return total

    rows_iota = lax.broadcasted_iota(jnp.int32, (width, width), 0)
    for i in range(2):
        turn[i] = (face_map[i : i + 1, :] == rows_iota).astype(f32)

    base[0:8, :] = jnp.broadcast_to(stiff[...], (8, stiff.shape[-1]))
    load_copies[0].wait()
    for f in (0, 2):
        base[:, cols[f]] = dot(base[:, cols[f]], turn[f // 2], (1, 1), highest)
    base_parts = [slice(0 if c == 0 else 8 + c * chunk, 8 + (c + 1) * chunk) for c in range(CHUNKS)]
    pl.semaphore_wait(barrier, subs + locs - 2)
    for c in range(CHUNKS):
        for f in range(4):
            face(base, received0, 0, c, f, base_parts[c]).send()

    def named(row, count):
        shape = (count, row.shape[-1])
        return (row == lax.broadcasted_iota(jnp.int32, shape, 0)).astype(f32)

    corner_hot = named(corner[...], level2_count)
    basis_copies = []
    for f in range(4):
        part = dot(corner_hot, basis[:, cols[f]], precision=highest)
        if f in (0, 2):
            part = dot(part, turn[f // 2], (1, 1), highest)
        group_basis[f] = part
        basis_copies.append(
            Neighbour(f, group_basis.at[f], lambda at: basis_in.at[at], basis_send, basis_recv)
        )
        basis_copies[f].send()
    level3_scatter[...] = named(level3_map[...], level3_count) * level3_weight[...]
    scatter_copies = [
        Neighbour(f, level3_scatter, lambda at: scatter_in.at[at], scatter_send, scatter_recv)
        for f in (0, 1)
    ]
    for copy in scatter_copies:
        copy.send()
    owner_hot = named(owner[...], max(8, locs))
    masked_two = inverse_two[...] * dot(owner_hot, owner_hot, (0, 0))

    def reorder(source, target):
        for f in (0, 2):
            one_hot = turn[f // 2].astype(bf16)
            source[cols[f], :] = dot(one_hot, source[cols[f], :]).astype(bf16)
        for f in (0, 2):
            one_hot = turn[f // 2].astype(bf16)
            target[:, cols[f]] = dot(source[:, cols[f]], one_hot, (1, 1)).astype(bf16)
        for f in (1, 3):
            target[:, cols[f]] = source[:, cols[f]]

    load_copies[1].wait()
    reorder(neumann_raw, neumann)
    load_copies[2].wait()
    reorder(schur_raw, schur)

    class Total:
        def __init__(self, i, tile):
            self.i = i
            scalar_loc[i, me_loc] = tile
            self.wait = spread("loc", scalar_loc.at[i], sl_send.at[i], sl_recv.at[i])

        def cross(self):
            self.wait()
            i = self.i
            scalar_sub[i, me_sub] = total_of(scalar_loc.at[i], locs)
            self.wait = spread("sub", scalar_sub.at[i], ss_send.at[i], ss_recv.at[i])

        def value(self):
            self.wait()
            return jnp.sum(total_of(scalar_sub.at[self.i], subs))

    def first_residual(c):
        for f in order:
            r[rows[c], cols[f]] = base[8 + c * chunk : 8 + (c + 1) * chunk, cols[f]]
            if c == 0:
                weight[:, cols[f]] = base[0:8, cols[f]]

            def add(f=f):
                start = 8 + c * chunk
                r[rows[c], cols[f]] += received0[f, start : start + chunk]
                if c == 0:
                    weight[:, cols[f]] += received0[f, 0:8]

            face(base, received0, 0, c, f, base_parts[c]).receive(add)
            if c == 0:
                weight[:, cols[f]] = base[0:8, cols[f]] / weight[:, cols[f]]
                part = group_basis[f] * weight[0:1, cols[f]]
                weighted_basis[:, cols[f]] = part

    def join_bases():
        for f in range(4):
            joint_basis[:, cols[f]] = weighted_basis[:, cols[f]]

            def join(f=f):
                scale = 1.0 - weight[0:1, cols[f]]
                basis_in[f] = basis_in[f] * scale
                if f >= 2:
                    joint_basis[:, cols[f]] += basis_in[f]

            basis_copies[f].receive(join)
        for copy in scatter_copies:
            copy.receive(lambda: None)

    def precondition(k, e, residual_rows, target):
        z = fields.at[e - 1]
        slots = received.at[e - 1]
        tile = jnp.zeros((8, 128), f32)
        for c in range(CHUNKS):
            residual_rows(c)
            level2 = jnp.zeros((level2_count, chunk), f32)
            for f in range(4):
                block = r[rows[c], cols[f]]
                rounded[rows[c], cols[f]] = (weight[0:1, cols[f]] * block).astype(bf16)
                level2 += dot(weighted_basis[:, cols[f]], block, (1, 1), highest)
            level2_parts[k, me_loc, :, rows[c]] = level2
            if c == CHUNKS - 1:
                wait = spread("loc", level2_parts.at[k], l2_send.at[k], l2_recv.at[k])
            for f in range(4):
                part = dot(rounded[rows[c], :], neumann[:, cols[f]]) * weight[0:1, cols[f]]
                z[rows[c], cols[f]] = part
                face(z, slots, e, c, f, rows[c]).send()
                tile += tile_sum(part * r[rows[c], cols[f]])
        wait()
        level2 = total_of(level2_parts.at[k], locs)
        share = level3_count // locs
        mine = level3_scatter[pl.ds(pl.multiple_of(me_loc * share, 8), share), :]
        level3_parts[k, me_sub] = dot(mine, level2, precision=highest)
        wait = spread("sub", level3_parts.at[k], l3_send.at[k], l3_recv.at[k])
        owned = dot(masked_two, level2, precision=highest)
        owned_mine[k] = owned
        owned_copies = [
            Neighbour(
                f,
                owned_mine.at[k],
                lambda at: owned_in.at[k, at],
                owned_send.at[k],
                owned_recv.at[k],
            )
            for f in (0, 1)
        ]
        for copy in owned_copies:
            copy.send()
        going = Total(2 * k, tile + tile_sum(owned * level2_parts[k, me_loc]))
        if k == 0:
            join_bases()
        wait()
        level3_rows[k, me_loc] = total_of(level3_parts.at[k], subs)
        wait = spread("loc", level3_rows.at[k], rows_send.at[k], rows_recv.at[k])
        going.cross()
        wait()
        level3 = level3_rows[k].reshape(level3_count, loads)
        level3_update = dot(inverse_three[...], level3, precision=highest)
        level3_inner = jnp.sum(level3 * level3_update)
        owned_mine_update = owned + dot(level3_scatter[...], level3_update, (0, 0), highest)
        for f in order:
            target[:, cols[f]] = z[:, cols[f]] + dot(
                owned_mine_update, joint_basis[:, cols[f]], (0, 0), highest
            )
        for f in (0, 1):

            def beside(f=f):
                update = owned_in[k, f] + dot(scatter_in[f], level3_update, (0, 0), highest)
                target[:, cols[f]] += dot(update, basis_in[f], (0, 0), highest)

            owned_copies[f].receive(beside)
        return going.value() + level3_inner

    def take_direction(c, e, target):
        for f in order:

            def add(f=f):
                target[rows[c], cols[f]] += received[e - 1, f, rows[c]]

            z = fields.at[e - 1]
            face(z, received.at[e - 1], e, c, f, rows[c]).receive(add)

    current = None
    residual_rows = first_residual
    out_copies = []
    for k in range(ITERS):
        e = 1 + 2 * k
        target = direction if k == 0 else direction2
        following = precondition(k, e, residual_rows, target)
        if k > 0:
            ratio = following / current
            for f in order:
                target[:, cols[f]] += ratio * direction[:, cols[f]]
        current = following
        image = fields.at[e]
        tile = jnp.zeros((8, 128), f32)
        for c in range(CHUNKS):
            take_direction(c, e, target)
            for f in range(4):
                rounded[rows[c], cols[f]] = target[rows[c], cols[f]].astype(bf16)
            for f in range(4):
                part = dot(rounded[rows[c], :], schur[:, cols[f]])
                image[rows[c], cols[f]] = part
                face(image, received.at[e], e + 1, c, f, rows[c]).send()
                tile += tile_sum(part * target[rows[c], cols[f]])
        going = Total(2 * k + 1, tile)
        going.cross()
        step = current / going.value()
        last = k + 1 == ITERS
        for f in order:
            part = step * target[:, cols[f]]
            if k > 0:
                part += solved[:, cols[f]]
            if last and f in (0, 2):
                part = dot(part, turn[f // 2], precision=highest)
            solved[:, cols[f]] = part
        if last:
            out_copies.append(pltpu.make_async_copy(solved, solution_out, out_sem.at[0]))
            out_copies[-1].start()

        def residual_rows(c, image=image, step=step, e=e):
            for f in order:
                r[rows[c], cols[f]] -= step * image[rows[c], cols[f]]

                def subtract(f=f):
                    r[rows[c], cols[f]] -= step * received[e, f, rows[c]]

                face(image, received.at[e], e + 1, c, f, rows[c]).receive(subtract)

    for c in range(CHUNKS):
        residual_rows(c)
        for f in (0, 2):
            r[rows[c], cols[f]] = dot(r[rows[c], cols[f]], turn[f // 2], precision=highest)
        out_copies.append(
            pltpu.make_async_copy(r.at[rows[c]], residual_out.at[rows[c]], out_sem.at[1 + c])
        )
        out_copies[-1].start()

    for finish in pending:
        finish()
    for copy in out_copies:
        copy.wait()


def on_device(mesh, *operands):
    subs, locs = mesh.shape["sub"], mesh.shape["loc"]
    (
        load_cases,
        schur_matrix,
        neumann,
        stiffness,
        face_map,
        basis,
        corner_map,
        owner_map,
        level2_inverse,
        level3_map,
        level3_weight,
        level3_inverse,
    ) = operands
    loads, order = load_cases.shape[1:]
    width = face_map.shape[-1]
    level2_count = level2_inverse.shape[-1]
    level3_count = level3_inverse.shape[-1]
    share = level3_count // locs
    vmem = pl.BlockSpec(memory_space=pltpu.VMEM)
    hbm = pl.BlockSpec(memory_space=pl.ANY)
    dma = pltpu.SemaphoreType.DMA
    field = jax.ShapeDtypeStruct((loads, order), f32)
    extra = EXCHANGES - 1
    totals = 2 * ITERS
    scratch = [
        pltpu.VMEM((loads + 8, order), f32),
        pltpu.VMEM((4, loads + 8, width), f32),
        pltpu.VMEM((extra, 4, loads, width), f32),
        pltpu.VMEM((order, order), bf16),
        pltpu.VMEM((order, order), bf16),
        pltpu.VMEM((order, order), bf16),
        pltpu.VMEM((order, order), bf16),
        pltpu.VMEM((2, width, width), f32),
        pltpu.VMEM((8, order), f32),
        pltpu.VMEM((4, level2_count, width), f32),
        pltpu.VMEM((level2_count, order), f32),
        pltpu.VMEM((level2_count, order), f32),
        pltpu.VMEM((4, level2_count, width), f32),
        pltpu.VMEM((level3_count, level2_count), f32),
        pltpu.VMEM((2, level3_count, level2_count), f32),
        pltpu.VMEM((ITERS, level2_count, loads), f32),
        pltpu.VMEM((ITERS, 2, level2_count, loads), f32),
        pltpu.VMEM((loads, order), f32),
        pltpu.VMEM((extra, loads, order), f32),
        pltpu.VMEM((loads, order), bf16),
        pltpu.VMEM((loads, order), f32),
        pltpu.VMEM((loads, order), f32),
        pltpu.VMEM((loads, order), f32),
        pltpu.VMEM((ITERS, locs, level2_count, loads), f32),
        pltpu.VMEM((ITERS, subs, share, loads), f32),
        pltpu.VMEM((ITERS, locs, share, loads), f32),
        pltpu.VMEM((totals, locs, 8, 128), f32),
        pltpu.VMEM((totals, subs, 8, 128), f32),
        dma((3,)),
        dma((1 + CHUNKS,)),
        dma((EXCHANGES, CHUNKS, 4)),
        dma((EXCHANGES, CHUNKS, 4)),
        dma((4,)),
        dma((4,)),
        dma((2,)),
        dma((2,)),
        dma((ITERS, 2)),
        dma((ITERS, 2)),
        dma((ITERS, locs)),
        dma((ITERS, locs)),
        dma((ITERS, subs)),
        dma((ITERS, subs)),
        dma((ITERS, locs)),
        dma((ITERS, locs)),
        dma((totals, locs)),
        dma((totals, locs)),
        dma((totals, subs)),
        dma((totals, subs)),
    ]
    outputs = pl.pallas_call(
        functools.partial(kernel, subs, locs),
        out_shape=(field, field),
        in_specs=[hbm] * 3 + [vmem] * 9,
        out_specs=(hbm, hbm),
        scratch_shapes=scratch,
        compiler_params=pltpu.CompilerParams(
            collective_id=0, has_side_effects=True, vmem_limit_bytes=56 * 1024 * 1024
        ),
    )(
        load_cases[0],
        schur_matrix[0],
        neumann[0],
        stiffness,
        face_map[0],
        basis[0].T,
        corner_map,
        owner_map,
        level2_inverse[0],
        level3_map,
        level3_weight,
        level3_inverse,
    )
    return tuple(value[None] for value in outputs)


def solution(mesh):
    both = ("sub", "loc")
    cube, flat = P(both, None, None), P(both, None)
    group, group_cube = P("sub", None), P("sub", None, None)
    placed = (cube, cube, cube, flat, cube, cube, flat, group, group_cube, group, group, P())
    return jax.shard_map(
        functools.partial(on_device, mesh),
        mesh=mesh,
        in_specs=placed,
        out_specs=(cube, cube),
        check_vma=False,
    )
```

```python
import functools

import jax
import jax.numpy as jnp
from jax import lax
from jax.experimental import pallas as pl
from jax.experimental.pallas import tpu as pltpu
from jax.sharding import PartitionSpec as P

ITERS = 2
EXCHANGES = 1 + 2 * ITERS
CHUNKS = 2
MESH = pl.DeviceIdType.MESH
highest = lax.Precision.HIGHEST
f32 = jnp.float32
bf16 = jnp.bfloat16


def dot(a, b, contract=(1, 0), precision=None):
    return lax.dot_general(
        a,
        b,
        (((contract[0],), (contract[1],)), ((), ())),
        precision=precision,
        preferred_element_type=f32,
    )


def tile_sum(block):
    rows, cols = block.shape
    folded = jnp.sum(block.reshape(rows // 8, 8, cols), axis=0)
    total = folded[:, :128]
    for start in range(128, cols, 128):
        total = total + folded[:, start : start + 128]
    return total


def kernel(
    subs,
    locs,
    load_hbm,
    schur_hbm,
    neumann_hbm,
    stiff,
    face_map,
    basis,
    corner,
    owner,
    inverse_two,
    level3_map,
    level3_weight,
    inverse_three,
    solution_out,
    residual_out,
    base,
    received0,
    received,
    schur,
    neumann,
    schur_raw,
    neumann_raw,
    turn,
    weight,
    group_basis,
    weighted_basis,
    joint_basis,
    basis_in,
    level3_scatter,
    scatter_in,
    owned_mine,
    owned_in,
    beside_mine,
    beside_in,
    level2_kept,
    owned_kept,
    level3_kept,
    r,
    fields,
    rounded,
    direction,
    direction2,
    solved,
    level2_parts,
    level3_parts,
    level3_rows,
    scalar_loc,
    scalar_sub,
    load_sem,
    out_sem,
    face_send,
    face_recv,
    basis_send,
    basis_recv,
    scatter_send,
    scatter_recv,
    owned_send,
    owned_recv,
    beside_send,
    beside_recv,
    l2_send,
    l2_recv,
    l3_send,
    l3_recv,
    rows_send,
    rows_recv,
    sl_send,
    sl_recv,
    ss_send,
    ss_recv,
):
    me_sub, me_loc = lax.axis_index("sub"), lax.axis_index("loc")
    loads = load_hbm.shape[0]
    width = face_map.shape[-1]
    level2_count = inverse_two.shape[-1]
    level3_count = inverse_three.shape[-1]
    cols = [slice(f * width, (f + 1) * width) for f in range(4)]
    chunk = loads // CHUNKS
    rows = [slice(c * chunk, (c + 1) * chunk) for c in range(CHUNKS)]
    order = (2, 3, 0, 1)

    load_copies = [
        pltpu.make_async_copy(load_hbm, base.at[pl.ds(8, loads)], load_sem.at[0]),
        pltpu.make_async_copy(neumann_hbm, neumann_raw, load_sem.at[1]),
        pltpu.make_async_copy(schur_hbm, schur_raw, load_sem.at[2]),
    ]
    for copy in load_copies:
        copy.start()

    barrier = pltpu.get_barrier_semaphore()
    for axis, count, me in (("sub", subs, me_sub), ("loc", locs, me_loc)):
        for d in range(1, count):
            pl.semaphore_signal(
                barrier,
                inc=1,
                device_id={axis: lax.rem(me + d, count)},
                device_id_type=MESH,
            )

    present = (me_sub > 0, me_sub < subs - 1, me_loc > 0, me_loc < locs - 1)
    partner = (
        {"sub": jnp.maximum(me_sub - 1, 0)},
        {"sub": jnp.minimum(me_sub + 1, subs - 1)},
        {"loc": jnp.maximum(me_loc - 1, 0)},
        {"loc": jnp.minimum(me_loc + 1, locs - 1)},
    )
    pending = []

    class Neighbour:
        def __init__(self, f, source, slot, send_sem, recv_sem):
            self.f = f
            self.make = lambda at: pltpu.make_async_remote_copy(
                src_ref=source,
                dst_ref=slot(at),
                send_sem=send_sem.at[f],
                recv_sem=recv_sem.at[at],
                device_id=partner[f],
                device_id_type=MESH,
            )

        def send(self):
            @pl.when(present[self.f])
            def _():
                self.make(self.f ^ 1).start()

            def finish():
                @pl.when(present[self.f])
                def _():
                    self.make(self.f ^ 1).wait_send()

            pending.append(finish)

        def receive(self, then):
            @pl.when(present[self.f])
            def _():
                self.make(self.f).wait_recv()
                then()

    def face(field, slots, e, c, f, part):
        return Neighbour(
            f,
            field.at[part, cols[f]],
            lambda at: slots.at[at, part],
            face_send.at[e, c],
            face_recv.at[e, c],
        )

    def spread(axis, slots, send_sem, recv_sem):
        count, me = (subs, me_sub) if axis == "sub" else (locs, me_loc)

        def make(d, slot):
            peer = lax.rem(me + d, count)
            slot = me if slot is None else peer
            return pltpu.make_async_remote_copy(
                src_ref=slots.at[me],
                dst_ref=slots.at[slot],
                send_sem=send_sem.at[d - 1],
                recv_sem=recv_sem.at[slot],
                device_id={axis: peer},
                device_id_type=MESH,
            )

        for d in range(1, count):
            make(d, None).start()

        def finish():
            for d in range(1, count):
                make(d, None).wait_send()

        pending.append(finish)

        def wait():
            for d in range(1, count):
                make(d, "peer").wait_recv()

        return wait

    def total_of(slots, count):
        total = slots[0]
        for i in range(1, count):
            total = total + slots[i]
        return total

    rows_iota = lax.broadcasted_iota(jnp.int32, (width, width), 0)
    for i in range(2):
        turn[i] = (face_map[i : i + 1, :] == rows_iota).astype(f32)

    base[0:8, :] = jnp.broadcast_to(stiff[...], (8, stiff.shape[-1]))
    load_copies[0].wait()
    for f in (0, 2):
        base[:, cols[f]] = dot(base[:, cols[f]], turn[f // 2], (1, 1), highest)
    base_parts = [slice(0 if c == 0 else 8 + c * chunk, 8 + (c + 1) * chunk) for c in range(CHUNKS)]
    pl.semaphore_wait(barrier, subs + locs - 2)

    def named(row, count):
        shape = (count, row.shape[-1])
        return (row == lax.broadcasted_iota(jnp.int32, shape, 0)).astype(f32)

    corner_hot = named(corner[...], level2_count)
    basis_copies = []
    for f in range(4):
        part = dot(corner_hot, basis[:, cols[f]], precision=highest)
        if f in (0, 2):
            part = dot(part, turn[f // 2], (1, 1), highest)
        group_basis[f] = part
        basis_copies.append(
            Neighbour(f, group_basis.at[f], lambda at: basis_in.at[at], basis_send, basis_recv)
        )
        basis_copies[f].send()
    level3_scatter[...] = named(level3_map[...], level3_count) * level3_weight[...]
    scatter_copies = [
        Neighbour(f, level3_scatter, lambda at: scatter_in.at[at], scatter_send, scatter_recv)
        for f in (0, 1)
    ]
    for copy in scatter_copies:
        copy.send()
    for c in range(CHUNKS):
        for f in range(4):
            face(base, received0, 0, c, f, base_parts[c]).send()
    owner_hot = named(owner[...], max(8, locs))
    masked_two = inverse_two[...] * dot(owner_hot, owner_hot, (0, 0))

    def reorder(source, target):
        for f in (0, 2):
            one_hot = turn[f // 2].astype(bf16)
            source[cols[f], :] = dot(one_hot, source[cols[f], :]).astype(bf16)
        for f in (0, 2):
            one_hot = turn[f // 2].astype(bf16)
            target[:, cols[f]] = dot(source[:, cols[f]], one_hot, (1, 1)).astype(bf16)
        for f in (1, 3):
            target[:, cols[f]] = source[:, cols[f]]

    load_copies[1].wait()
    reorder(neumann_raw, neumann)
    load_copies[2].wait()
    reorder(schur_raw, schur)

    class Total:
        def __init__(self, i, tile):
            self.i = i
            scalar_loc[i, me_loc] = tile
            self.wait = spread("loc", scalar_loc.at[i], sl_send.at[i], sl_recv.at[i])

        def cross(self):
            self.wait()
            i = self.i
            scalar_sub[i, me_sub] = total_of(scalar_loc.at[i], locs)
            self.wait = spread("sub", scalar_sub.at[i], ss_send.at[i], ss_recv.at[i])

        def value(self):
            self.wait()
            return jnp.sum(total_of(scalar_sub.at[self.i], subs))

    def first_residual(c):
        for f in order:
            r[rows[c], cols[f]] = base[8 + c * chunk : 8 + (c + 1) * chunk, cols[f]]
            if c == 0:
                weight[:, cols[f]] = base[0:8, cols[f]]

            def add(f=f):
                start = 8 + c * chunk
                r[rows[c], cols[f]] += received0[f, start : start + chunk]
                if c == 0:
                    weight[:, cols[f]] += received0[f, 0:8]

            face(base, received0, 0, c, f, base_parts[c]).receive(add)
            if c == 0:
                weight[:, cols[f]] = base[0:8, cols[f]] / weight[:, cols[f]]
                part = group_basis[f] * weight[0:1, cols[f]]
                weighted_basis[:, cols[f]] = part

    def join_bases():
        for f in range(4):
            joint_basis[:, cols[f]] = weighted_basis[:, cols[f]]

            def join(f=f):
                scale = 1.0 - weight[0:1, cols[f]]
                basis_in[f] = basis_in[f] * scale
                if f >= 2:
                    joint_basis[:, cols[f]] += basis_in[f]

            basis_copies[f].receive(join)
        for copy in scatter_copies:
            copy.receive(lambda: None)

    share = level3_count // locs

    class Coarse:
        def __init__(self, k, block):
            part = jnp.zeros((level2_count, loads), f32)
            for f in range(4):
                part += dot(joint_basis[:, cols[f]], block(f), (1, 1), highest)
            level2_parts[k, me_loc] = part
            beside = []
            for f in (0, 1):

                @pl.when(present[f])
                def _(f=f):
                    beside_mine[k, f] = dot(basis_in[f], block(f), (1, 1), highest)

                beside.append(
                    Neighbour(
                        f,
                        beside_mine.at[k, f],
                        lambda at: beside_in.at[k, at],
                        beside_send.at[k],
                        beside_recv.at[k],
                    )
                )
                beside[f].send()
            self.k, self.beside = k, beside

        def group(self):
            k = self.k
            for f in (0, 1):

                def add(f=f):
                    level2_parts[k, me_loc] += beside_in[k, f]

                self.beside[f].receive(add)
            self.wait = spread("loc", level2_parts.at[k], l2_send.at[k], l2_recv.at[k])

        def cross(self):
            k = self.k
            self.wait()
            self.level2 = total_of(level2_parts.at[k], locs)
            mine = level3_scatter[pl.ds(pl.multiple_of(me_loc * share, 8), share), :]
            level3_parts[k, me_sub] = dot(mine, self.level2, precision=highest)
            self.wait = spread("sub", level3_parts.at[k], l3_send.at[k], l3_recv.at[k])
            self.owned = dot(masked_two, self.level2, precision=highest)
            owned_mine[k] = self.owned
            self.copies = [
                Neighbour(
                    f,
                    owned_mine.at[k],
                    lambda at: owned_in.at[k, at],
                    owned_send.at[k],
                    owned_recv.at[k],
                )
                for f in (0, 1)
            ]
            for copy in self.copies:
                copy.send()

        def gather(self):
            k = self.k
            self.wait()
            level3_rows[k, me_loc] = total_of(level3_parts.at[k], subs)
            self.wait = spread("loc", level3_rows.at[k], rows_send.at[k], rows_recv.at[k])

        def finish(self):
            self.wait()
            self.level3 = level3_rows[self.k].reshape(level3_count, loads)

    coarse = []

    def precondition(k, e, residual_rows, target, step):
        z = fields.at[e - 1]
        slots = received.at[e - 1]
        tile = jnp.zeros((8, 128), f32)
        for c in range(CHUNKS):
            residual_rows(c)
            for f in range(4):
                block = r[rows[c], cols[f]]
                rounded[rows[c], cols[f]] = (weight[0:1, cols[f]] * block).astype(bf16)
            if k == 0 and c == 0:
                join_bases()
                coarse.append(Coarse(0, lambda f: base[8:, cols[f]]))
            for f in range(4):
                part = dot(rounded[rows[c], :], neumann[:, cols[f]]) * weight[0:1, cols[f]]
                z[rows[c], cols[f]] = part
                face(z, slots, e, c, f, rows[c]).send()
                tile += tile_sum(part * r[rows[c], cols[f]])
            if k == 0 and c == 0:
                coarse[0].group()
                coarse[0].cross()
        last = coarse[-1]
        last.gather()
        level2, owned = last.level2, last.owned
        if k > 0:
            level2 = level2_kept[...] - step * level2
            owned = owned_kept[...] - step * owned
        level2_kept[...] = level2
        owned_kept[...] = owned
        going = Total(2 * k, tile + tile_sum(owned * level2) * (1.0 / locs))
        last.finish()
        level3 = last.level3
        if k > 0:
            level3 = level3_kept[...] - step * level3
        level3_kept[...] = level3
        going.cross()
        level3_update = dot(inverse_three[...], level3, precision=highest)
        level3_inner = jnp.sum(level3 * level3_update)
        update = owned + dot(level3_scatter[...], level3_update, (0, 0), highest)
        for f in order:
            target[:, cols[f]] = z[:, cols[f]] + dot(
                update, joint_basis[:, cols[f]], (0, 0), highest
            )
        for f in (0, 1):

            def beside(f=f):
                theirs = owned_in[k, f]
                if k > 0:
                    theirs = owned_in[k - 1, f] - step * theirs
                    owned_in[k, f] = theirs
                theirs += dot(scatter_in[f], level3_update, (0, 0), highest)
                target[:, cols[f]] += dot(theirs, basis_in[f], (0, 0), highest)

            last.copies[f].receive(beside)
        return going.value() + level3_inner

    def take_direction(c, e, target):
        for f in order:

            def add(f=f):
                target[rows[c], cols[f]] += received[e - 1, f, rows[c]]

            z = fields.at[e - 1]
            face(z, received.at[e - 1], e, c, f, rows[c]).receive(add)

    current = None
    step = None
    residual_rows = first_residual
    out_copies = []
    for k in range(ITERS):
        e = 1 + 2 * k
        target = direction if k == 0 else direction2
        following = precondition(k, e, residual_rows, target, step)
        if k > 0:
            ratio = following / current
            for f in order:
                target[:, cols[f]] += ratio * direction[:, cols[f]]
        current = following
        image = fields.at[e]
        tile = jnp.zeros((8, 128), f32)
        for c in range(CHUNKS):
            take_direction(c, e, target)
            for f in range(4):
                rounded[rows[c], cols[f]] = target[rows[c], cols[f]].astype(bf16)
            for f in range(4):
                part = dot(rounded[rows[c], :], schur[:, cols[f]])
                image[rows[c], cols[f]] = part
                face(image, received.at[e], e + 1, c, f, rows[c]).send()
                tile += tile_sum(part * target[rows[c], cols[f]])
        going = Total(2 * k + 1, tile)
        last = k + 1 == ITERS
        if not last:
            coarse.append(Coarse(k + 1, lambda f, image=image: image[:, cols[f]]))
        going.cross()
        if not last:
            coarse[-1].group()
            coarse[-1].cross()
        step = current / going.value()
        for f in order:
            part = step * target[:, cols[f]]
            if k > 0:
                part += solved[:, cols[f]]
            if last and f in (0, 2):
                part = dot(part, turn[f // 2], precision=highest)
            solved[:, cols[f]] = part
        if last:
            out_copies.append(pltpu.make_async_copy(solved, solution_out, out_sem.at[0]))
            out_copies[-1].start()

        def residual_rows(c, image=image, step=step, e=e):
            for f in order:
                r[rows[c], cols[f]] -= step * image[rows[c], cols[f]]

                def subtract(f=f):
                    r[rows[c], cols[f]] -= step * received[e, f, rows[c]]

                face(image, received.at[e], e + 1, c, f, rows[c]).receive(subtract)

    for c in range(CHUNKS):
        residual_rows(c)
        for f in (0, 2):
            r[rows[c], cols[f]] = dot(r[rows[c], cols[f]], turn[f // 2], precision=highest)
        out_copies.append(
            pltpu.make_async_copy(r.at[rows[c]], residual_out.at[rows[c]], out_sem.at[1 + c])
        )
        out_copies[-1].start()

    for finish in pending:
        finish()
    for copy in out_copies:
        copy.wait()


def on_device(mesh, *operands):
    subs, locs = mesh.shape["sub"], mesh.shape["loc"]
    (
        load_cases,
        schur_matrix,
        neumann,
        stiffness,
        face_map,
        basis,
        corner_map,
        owner_map,
        level2_inverse,
        level3_map,
        level3_weight,
        level3_inverse,
    ) = operands
    loads, order = load_cases.shape[1:]
    width = face_map.shape[-1]
    level2_count = level2_inverse.shape[-1]
    level3_count = level3_inverse.shape[-1]
    share = level3_count // locs
    vmem = pl.BlockSpec(memory_space=pltpu.VMEM)
    hbm = pl.BlockSpec(memory_space=pl.ANY)
    dma = pltpu.SemaphoreType.DMA
    field = jax.ShapeDtypeStruct((loads, order), f32)
    extra = EXCHANGES - 1
    totals = 2 * ITERS
    scratch = [
        pltpu.VMEM((loads + 8, order), f32),
        pltpu.VMEM((4, loads + 8, width), f32),
        pltpu.VMEM((extra, 4, loads, width), f32),
        pltpu.VMEM((order, order), bf16),
        pltpu.VMEM((order, order), bf16),
        pltpu.VMEM((order, order), bf16),
        pltpu.VMEM((order, order), bf16),
        pltpu.VMEM((2, width, width), f32),
        pltpu.VMEM((8, order), f32),
        pltpu.VMEM((4, level2_count, width), f32),
        pltpu.VMEM((level2_count, order), f32),
        pltpu.VMEM((level2_count, order), f32),
        pltpu.VMEM((4, level2_count, width), f32),
        pltpu.VMEM((level3_count, level2_count), f32),
        pltpu.VMEM((2, level3_count, level2_count), f32),
        pltpu.VMEM((ITERS, level2_count, loads), f32),
        pltpu.VMEM((ITERS, 2, level2_count, loads), f32),
        pltpu.VMEM((ITERS, 2, level2_count, loads), f32),
        pltpu.VMEM((ITERS, 2, level2_count, loads), f32),
        pltpu.VMEM((level2_count, loads), f32),
        pltpu.VMEM((level2_count, loads), f32),
        pltpu.VMEM((level3_count, loads), f32),
        pltpu.VMEM((loads, order), f32),
        pltpu.VMEM((extra, loads, order), f32),
        pltpu.VMEM((loads, order), bf16),
        pltpu.VMEM((loads, order), f32),
        pltpu.VMEM((loads, order), f32),
        pltpu.VMEM((loads, order), f32),
        pltpu.VMEM((ITERS, locs, level2_count, loads), f32),
        pltpu.VMEM((ITERS, subs, share, loads), f32),
        pltpu.VMEM((ITERS, locs, share, loads), f32),
        pltpu.VMEM((totals, locs, 8, 128), f32),
        pltpu.VMEM((totals, subs, 8, 128), f32),
        dma((3,)),
        dma((1 + CHUNKS,)),
        dma((EXCHANGES, CHUNKS, 4)),
        dma((EXCHANGES, CHUNKS, 4)),
        dma((4,)),
        dma((4,)),
        dma((2,)),
        dma((2,)),
        dma((ITERS, 2)),
        dma((ITERS, 2)),
        dma((ITERS, 2)),
        dma((ITERS, 2)),
        dma((ITERS, locs)),
        dma((ITERS, locs)),
        dma((ITERS, subs)),
        dma((ITERS, subs)),
        dma((ITERS, locs)),
        dma((ITERS, locs)),
        dma((totals, locs)),
        dma((totals, locs)),
        dma((totals, subs)),
        dma((totals, subs)),
    ]
    outputs = pl.pallas_call(
        functools.partial(kernel, subs, locs),
        out_shape=(field, field),
        in_specs=[hbm] * 3 + [vmem] * 9,
        out_specs=(hbm, hbm),
        scratch_shapes=scratch,
        compiler_params=pltpu.CompilerParams(
            collective_id=0, has_side_effects=True, vmem_limit_bytes=56 * 1024 * 1024
        ),
    )(
        load_cases[0],
        schur_matrix[0],
        neumann[0],
        stiffness,
        face_map[0],
        basis[0].T,
        corner_map,
        owner_map,
        level2_inverse[0],
        level3_map,
        level3_weight,
        level3_inverse,
    )
    return tuple(value[None] for value in outputs)


def solution(mesh):
    both = ("sub", "loc")
    cube, flat = P(both, None, None), P(both, None)
    group, group_cube = P("sub", None), P("sub", None, None)
    placed = (cube, cube, cube, flat, cube, cube, flat, group, group_cube, group, group, P())
    return jax.shard_map(
        functools.partial(on_device, mesh),
        mesh=mesh,
        in_specs=placed,
        out_specs=(cube, cube),
        check_vma=False,
    )
```

```python
import functools

import jax
import jax.numpy as jnp
from jax import lax
from jax.experimental import pallas as pl
from jax.experimental.pallas import tpu as pltpu
from jax.sharding import PartitionSpec as P

ITERS = 2
EXCHANGES = 1 + 2 * ITERS
CHUNKS = 2
MESH = pl.DeviceIdType.MESH
highest = lax.Precision.HIGHEST
f32 = jnp.float32
bf16 = jnp.bfloat16


def dot(a, b, contract=(1, 0), precision=None):
    return lax.dot_general(
        a,
        b,
        (((contract[0],), (contract[1],)), ((), ())),
        precision=precision,
        preferred_element_type=f32,
    )


def tile_sum(block):
    rows, cols = block.shape
    folded = jnp.sum(block.reshape(rows // 8, 8, cols), axis=0)
    total = folded[:, :128]
    for start in range(128, cols, 128):
        total = total + folded[:, start : start + 128]
    return total


def kernel(
    subs,
    locs,
    load_hbm,
    schur_hbm,
    neumann_hbm,
    stiff,
    face_map,
    basis,
    corner,
    owner,
    inverse_two,
    level3_map,
    level3_weight,
    inverse_three,
    solution_out,
    residual_out,
    base,
    received0,
    received,
    schur,
    neumann,
    schur_raw,
    neumann_raw,
    turn,
    weight,
    group_basis,
    weighted_basis,
    joint_basis,
    basis_in,
    level3_scatter,
    scatter_in,
    owned_mine,
    owned_in,
    beside_mine,
    beside_in,
    level2_kept,
    owned_kept,
    level3_kept,
    r,
    fields,
    rounded,
    direction,
    direction2,
    solved,
    level2_parts,
    level3_parts,
    level3_rows,
    scalar_loc,
    scalar_sub,
    load_sem,
    out_sem,
    face_send,
    face_recv,
    basis_send,
    basis_recv,
    scatter_send,
    scatter_recv,
    owned_send,
    owned_recv,
    beside_send,
    beside_recv,
    l2_send,
    l2_recv,
    l3_send,
    l3_recv,
    rows_send,
    rows_recv,
    sl_send,
    sl_recv,
    ss_send,
    ss_recv,
):
    me_sub, me_loc = lax.axis_index("sub"), lax.axis_index("loc")
    loads = load_hbm.shape[0]
    width = face_map.shape[-1]
    level2_count = inverse_two.shape[-1]
    level3_count = inverse_three.shape[-1]
    cols = [slice(f * width, (f + 1) * width) for f in range(4)]
    chunk = loads // CHUNKS
    rows = [slice(c * chunk, (c + 1) * chunk) for c in range(CHUNKS)]
    order = (2, 3, 0, 1)

    load_copies = [
        pltpu.make_async_copy(load_hbm, base.at[pl.ds(8, loads)], load_sem.at[0]),
        pltpu.make_async_copy(neumann_hbm, neumann_raw, load_sem.at[1]),
        pltpu.make_async_copy(schur_hbm, schur_raw, load_sem.at[2]),
    ]
    for copy in load_copies:
        copy.start()

    barrier = pltpu.get_barrier_semaphore()
    for axis, count, me in (("sub", subs, me_sub), ("loc", locs, me_loc)):
        for d in range(1, count):
            pl.semaphore_signal(
                barrier,
                inc=1,
                device_id={axis: lax.rem(me + d, count)},
                device_id_type=MESH,
            )

    present = (me_sub > 0, me_sub < subs - 1, me_loc > 0, me_loc < locs - 1)
    partner = (
        {"sub": jnp.maximum(me_sub - 1, 0)},
        {"sub": jnp.minimum(me_sub + 1, subs - 1)},
        {"loc": jnp.maximum(me_loc - 1, 0)},
        {"loc": jnp.minimum(me_loc + 1, locs - 1)},
    )
    pending = []

    class Neighbour:
        def __init__(self, f, source, slot, send_sem, recv_sem):
            self.f = f
            self.make = lambda at: pltpu.make_async_remote_copy(
                src_ref=source,
                dst_ref=slot(at),
                send_sem=send_sem.at[f],
                recv_sem=recv_sem.at[at],
                device_id=partner[f],
                device_id_type=MESH,
            )

        def send(self):
            @pl.when(present[self.f])
            def _():
                self.make(self.f ^ 1).start()

            def finish():
                @pl.when(present[self.f])
                def _():
                    self.make(self.f ^ 1).wait_send()

            pending.append(finish)

        def receive(self, then):
            @pl.when(present[self.f])
            def _():
                self.make(self.f).wait_recv()
                then()

    def face(field, slots, e, c, f, part):
        return Neighbour(
            f,
            field.at[part, cols[f]],
            lambda at: slots.at[at, part],
            face_send.at[e, c],
            face_recv.at[e, c],
        )

    def spread(axis, slots, send_sem, recv_sem):
        count, me = (subs, me_sub) if axis == "sub" else (locs, me_loc)

        def make(d, slot):
            peer = lax.rem(me + d, count)
            slot = me if slot is None else peer
            return pltpu.make_async_remote_copy(
                src_ref=slots.at[me],
                dst_ref=slots.at[slot],
                send_sem=send_sem.at[d - 1],
                recv_sem=recv_sem.at[slot],
                device_id={axis: peer},
                device_id_type=MESH,
            )

        for d in range(1, count):
            make(d, None).start()

        def finish():
            for d in range(1, count):
                make(d, None).wait_send()

        pending.append(finish)

        def wait():
            for d in range(1, count):
                make(d, "peer").wait_recv()

        return wait

    def total_of(slots, count):
        total = slots[0]
        for i in range(1, count):
            total = total + slots[i]
        return total

    rows_iota = lax.broadcasted_iota(jnp.int32, (width, width), 0)
    for i in range(2):
        turn[i] = (face_map[i : i + 1, :] == rows_iota).astype(f32)

    base[0:8, :] = jnp.broadcast_to(stiff[...], (8, stiff.shape[-1]))
    load_copies[0].wait()
    for f in (0, 2):
        base[:, cols[f]] = dot(base[:, cols[f]], turn[f // 2], (1, 1), highest)
    base_parts = [slice(0 if c == 0 else 8 + c * chunk, 8 + (c + 1) * chunk) for c in range(CHUNKS)]
    pl.semaphore_wait(barrier, subs + locs - 2)

    def named(row, count):
        shape = (count, row.shape[-1])
        return (row == lax.broadcasted_iota(jnp.int32, shape, 0)).astype(f32)

    corner_hot = named(corner[...], level2_count)
    basis_copies = []
    for f in range(4):
        part = dot(corner_hot, basis[:, cols[f]], precision=highest)
        if f in (0, 2):
            part = dot(part, turn[f // 2], (1, 1), highest)
        group_basis[f] = part
        basis_copies.append(
            Neighbour(f, group_basis.at[f], lambda at: basis_in.at[at], basis_send, basis_recv)
        )
        basis_copies[f].send()
    level3_scatter[...] = named(level3_map[...], level3_count) * level3_weight[...]
    scatter_copies = [
        Neighbour(f, level3_scatter, lambda at: scatter_in.at[at], scatter_send, scatter_recv)
        for f in (0, 1)
    ]
    for copy in scatter_copies:
        copy.send()
    for c in range(CHUNKS):
        for f in range(4):
            face(base, received0, 0, c, f, base_parts[c]).send()
    owner_hot = named(owner[...], max(8, locs))
    masked_two = inverse_two[...] * dot(owner_hot, owner_hot, (0, 0))

    def reorder(source, target):
        for f in (0, 2):
            one_hot = turn[f // 2].astype(bf16)
            source[cols[f], :] = dot(one_hot, source[cols[f], :]).astype(bf16)
        for f in (0, 2):
            one_hot = turn[f // 2].astype(bf16)
            target[:, cols[f]] = dot(source[:, cols[f]], one_hot, (1, 1)).astype(bf16)
        for f in (1, 3):
            target[:, cols[f]] = source[:, cols[f]]

    load_copies[1].wait()
    reorder(neumann_raw, neumann)
    load_copies[2].wait()
    reorder(schur_raw, schur)

    class Total:
        def __init__(self, i, tile):
            self.i = i
            scalar_loc[i, me_loc] = tile
            self.wait = spread("loc", scalar_loc.at[i], sl_send.at[i], sl_recv.at[i])

        def cross(self):
            self.wait()
            i = self.i
            scalar_sub[i, me_sub] = total_of(scalar_loc.at[i], locs)
            self.wait = spread("sub", scalar_sub.at[i], ss_send.at[i], ss_recv.at[i])

        def value(self):
            self.wait()
            return jnp.sum(total_of(scalar_sub.at[self.i], subs))

    def first_residual(c):
        for f in order:
            r[rows[c], cols[f]] = base[8 + c * chunk : 8 + (c + 1) * chunk, cols[f]]
            if c == 0:
                weight[:, cols[f]] = base[0:8, cols[f]]

            def add(f=f):
                start = 8 + c * chunk
                r[rows[c], cols[f]] += received0[f, start : start + chunk]
                if c == 0:
                    weight[:, cols[f]] += received0[f, 0:8]

            face(base, received0, 0, c, f, base_parts[c]).receive(add)
            if c == 0:
                weight[:, cols[f]] = base[0:8, cols[f]] / weight[:, cols[f]]
                part = group_basis[f] * weight[0:1, cols[f]]
                weighted_basis[:, cols[f]] = part

    def join_bases():
        for f in range(4):
            joint_basis[:, cols[f]] = weighted_basis[:, cols[f]]

            def join(f=f):
                scale = 1.0 - weight[0:1, cols[f]]
                basis_in[f] = basis_in[f] * scale
                if f >= 2:
                    joint_basis[:, cols[f]] += basis_in[f]

            basis_copies[f].receive(join)
        for copy in scatter_copies:
            copy.receive(lambda: None)

    share = level3_count // locs

    class Coarse:
        def __init__(self, k, block):
            part = jnp.zeros((level2_count, loads), f32)
            for f in range(4):
                part += dot(joint_basis[:, cols[f]], block(f), (1, 1), highest)
            level2_parts[k, me_loc] = part
            beside = []
            for f in (0, 1):

                @pl.when(present[f])
                def _(f=f):
                    beside_mine[k, f] = dot(basis_in[f], block(f), (1, 1), highest)

                beside.append(
                    Neighbour(
                        f,
                        beside_mine.at[k, f],
                        lambda at: beside_in.at[k, at],
                        beside_send.at[k],
                        beside_recv.at[k],
                    )
                )
                beside[f].send()
            self.k, self.beside = k, beside

        def group(self):
            k = self.k
            for f in (0, 1):

                def add(f=f):
                    level2_parts[k, me_loc] += beside_in[k, f]

                self.beside[f].receive(add)
            self.wait = spread("loc", level2_parts.at[k], l2_send.at[k], l2_recv.at[k])

        def cross(self):
            k = self.k
            self.wait()
            self.level2 = total_of(level2_parts.at[k], locs)
            mine = level3_scatter[pl.ds(pl.multiple_of(me_loc * share, 8), share), :]
            level3_parts[k, me_sub] = dot(mine, self.level2, precision=highest)
            self.wait = spread("sub", level3_parts.at[k], l3_send.at[k], l3_recv.at[k])
            self.owned = dot(masked_two, self.level2, precision=highest)
            owned_mine[k] = self.owned
            self.copies = [
                Neighbour(
                    f,
                    owned_mine.at[k],
                    lambda at: owned_in.at[k, at],
                    owned_send.at[k],
                    owned_recv.at[k],
                )
                for f in (0, 1)
            ]
            for copy in self.copies:
                copy.send()

        def gather(self):
            k = self.k
            self.wait()
            level3_rows[k, me_loc] = total_of(level3_parts.at[k], subs)
            self.wait = spread("loc", level3_rows.at[k], rows_send.at[k], rows_recv.at[k])

        def finish(self):
            self.wait()
            self.level3 = level3_rows[self.k].reshape(level3_count, loads)

    coarse = []

    def precondition(k, e, residual_rows, target, step):
        z = fields.at[e - 1]
        slots = received.at[e - 1]
        tile = jnp.zeros((8, 128), f32)
        for c in range(CHUNKS):
            residual_rows(c)
            for f in range(4):
                block = r[rows[c], cols[f]]
                rounded[rows[c], cols[f]] = (weight[0:1, cols[f]] * block).astype(bf16)
            if k == 0 and c == 0:
                join_bases()
                coarse.append(Coarse(0, lambda f: base[8:, cols[f]]))
            for f in range(4):
                part = dot(rounded[rows[c], :], neumann[:, cols[f]]) * weight[0:1, cols[f]]
                z[rows[c], cols[f]] = part
                face(z, slots, e, c, f, rows[c]).send()
                tile += tile_sum(part * r[rows[c], cols[f]])
            if k == 0 and c == 0:
                coarse[0].group()
            if c == (CHUNKS - 1 if k == 0 else 0):
                coarse[-1].cross()
        last = coarse[-1]
        last.gather()
        level2, owned = last.level2, last.owned
        if k > 0:
            level2 = level2_kept[...] - step * level2
            owned = owned_kept[...] - step * owned
        level2_kept[...] = level2
        owned_kept[...] = owned
        going = Total(2 * k, tile + tile_sum(owned * level2) * (1.0 / locs))
        last.finish()
        level3 = last.level3
        if k > 0:
            level3 = level3_kept[...] - step * level3
        level3_kept[...] = level3
        going.cross()
        level3_update = dot(inverse_three[...], level3, precision=highest)
        level3_inner = jnp.sum(level3 * level3_update)
        update = owned + dot(level3_scatter[...], level3_update, (0, 0), highest)
        for f in order:
            target[:, cols[f]] = z[:, cols[f]] + dot(
                update, joint_basis[:, cols[f]], (0, 0), highest
            )
        for f in (0, 1):

            def beside(f=f):
                theirs = owned_in[k, f]
                if k > 0:
                    theirs = owned_in[k - 1, f] - step * theirs
                    owned_in[k, f] = theirs
                theirs += dot(scatter_in[f], level3_update, (0, 0), highest)
                target[:, cols[f]] += dot(theirs, basis_in[f], (0, 0), highest)

            last.copies[f].receive(beside)
        return going.value() + level3_inner

    def take_direction(c, e, target):
        for f in order:

            def add(f=f):
                target[rows[c], cols[f]] += received[e - 1, f, rows[c]]

            z = fields.at[e - 1]
            face(z, received.at[e - 1], e, c, f, rows[c]).receive(add)

    current = None
    step = None
    residual_rows = first_residual
    out_copies = []
    for k in range(ITERS):
        e = 1 + 2 * k
        target = direction if k == 0 else direction2
        following = precondition(k, e, residual_rows, target, step)
        if k > 0:
            ratio = following / current
            for f in order:
                target[:, cols[f]] += ratio * direction[:, cols[f]]
        current = following
        image = fields.at[e]
        tile = jnp.zeros((8, 128), f32)
        for c in range(CHUNKS):
            take_direction(c, e, target)
            for f in range(4):
                rounded[rows[c], cols[f]] = target[rows[c], cols[f]].astype(bf16)
            for f in range(4):
                part = dot(rounded[rows[c], :], schur[:, cols[f]])
                image[rows[c], cols[f]] = part
                face(image, received.at[e], e + 1, c, f, rows[c]).send()
                tile += tile_sum(part * target[rows[c], cols[f]])
        going = Total(2 * k + 1, tile)
        last = k + 1 == ITERS
        if not last:
            coarse.append(Coarse(k + 1, lambda f, image=image: image[:, cols[f]]))
        going.cross()
        if not last:
            coarse[-1].group()
        step = current / going.value()
        for f in order:
            part = step * target[:, cols[f]]
            if k > 0:
                part += solved[:, cols[f]]
            if last and f in (0, 2):
                part = dot(part, turn[f // 2], precision=highest)
            solved[:, cols[f]] = part
        if last:
            out_copies.append(pltpu.make_async_copy(solved, solution_out, out_sem.at[0]))
            out_copies[-1].start()

        def residual_rows(c, image=image, step=step, e=e):
            for f in order:
                r[rows[c], cols[f]] -= step * image[rows[c], cols[f]]

                def subtract(f=f):
                    r[rows[c], cols[f]] -= step * received[e, f, rows[c]]

                face(image, received.at[e], e + 1, c, f, rows[c]).receive(subtract)

    for c in range(CHUNKS):
        residual_rows(c)
        for f in (0, 2):
            r[rows[c], cols[f]] = dot(r[rows[c], cols[f]], turn[f // 2], precision=highest)
        out_copies.append(
            pltpu.make_async_copy(r.at[rows[c]], residual_out.at[rows[c]], out_sem.at[1 + c])
        )
        out_copies[-1].start()

    for finish in pending:
        finish()
    for copy in out_copies:
        copy.wait()


def on_device(mesh, *operands):
    subs, locs = mesh.shape["sub"], mesh.shape["loc"]
    (
        load_cases,
        schur_matrix,
        neumann,
        stiffness,
        face_map,
        basis,
        corner_map,
        owner_map,
        level2_inverse,
        level3_map,
        level3_weight,
        level3_inverse,
    ) = operands
    loads, order = load_cases.shape[1:]
    width = face_map.shape[-1]
    level2_count = level2_inverse.shape[-1]
    level3_count = level3_inverse.shape[-1]
    share = level3_count // locs
    vmem = pl.BlockSpec(memory_space=pltpu.VMEM)
    hbm = pl.BlockSpec(memory_space=pl.ANY)
    dma = pltpu.SemaphoreType.DMA
    field = jax.ShapeDtypeStruct((loads, order), f32)
    extra = EXCHANGES - 1
    totals = 2 * ITERS
    scratch = [
        pltpu.VMEM((loads + 8, order), f32),
        pltpu.VMEM((4, loads + 8, width), f32),
        pltpu.VMEM((extra, 4, loads, width), f32),
        pltpu.VMEM((order, order), bf16),
        pltpu.VMEM((order, order), bf16),
        pltpu.VMEM((order, order), bf16),
        pltpu.VMEM((order, order), bf16),
        pltpu.VMEM((2, width, width), f32),
        pltpu.VMEM((8, order), f32),
        pltpu.VMEM((4, level2_count, width), f32),
        pltpu.VMEM((level2_count, order), f32),
        pltpu.VMEM((level2_count, order), f32),
        pltpu.VMEM((4, level2_count, width), f32),
        pltpu.VMEM((level3_count, level2_count), f32),
        pltpu.VMEM((2, level3_count, level2_count), f32),
        pltpu.VMEM((ITERS, level2_count, loads), f32),
        pltpu.VMEM((ITERS, 2, level2_count, loads), f32),
        pltpu.VMEM((ITERS, 2, level2_count, loads), f32),
        pltpu.VMEM((ITERS, 2, level2_count, loads), f32),
        pltpu.VMEM((level2_count, loads), f32),
        pltpu.VMEM((level2_count, loads), f32),
        pltpu.VMEM((level3_count, loads), f32),
        pltpu.VMEM((loads, order), f32),
        pltpu.VMEM((extra, loads, order), f32),
        pltpu.VMEM((loads, order), bf16),
        pltpu.VMEM((loads, order), f32),
        pltpu.VMEM((loads, order), f32),
        pltpu.VMEM((loads, order), f32),
        pltpu.VMEM((ITERS, locs, level2_count, loads), f32),
        pltpu.VMEM((ITERS, subs, share, loads), f32),
        pltpu.VMEM((ITERS, locs, share, loads), f32),
        pltpu.VMEM((totals, locs, 8, 128), f32),
        pltpu.VMEM((totals, subs, 8, 128), f32),
        dma((3,)),
        dma((1 + CHUNKS,)),
        dma((EXCHANGES, CHUNKS, 4)),
        dma((EXCHANGES, CHUNKS, 4)),
        dma((4,)),
        dma((4,)),
        dma((2,)),
        dma((2,)),
        dma((ITERS, 2)),
        dma((ITERS, 2)),
        dma((ITERS, 2)),
        dma((ITERS, 2)),
        dma((ITERS, locs)),
        dma((ITERS, locs)),
        dma((ITERS, subs)),
        dma((ITERS, subs)),
        dma((ITERS, locs)),
        dma((ITERS, locs)),
        dma((totals, locs)),
        dma((totals, locs)),
        dma((totals, subs)),
        dma((totals, subs)),
    ]
    outputs = pl.pallas_call(
        functools.partial(kernel, subs, locs),
        out_shape=(field, field),
        in_specs=[hbm] * 3 + [vmem] * 9,
        out_specs=(hbm, hbm),
        scratch_shapes=scratch,
        compiler_params=pltpu.CompilerParams(
            collective_id=0, has_side_effects=True, vmem_limit_bytes=56 * 1024 * 1024
        ),
    )(
        load_cases[0],
        schur_matrix[0],
        neumann[0],
        stiffness,
        face_map[0],
        basis[0].T,
        corner_map,
        owner_map,
        level2_inverse[0],
        level3_map,
        level3_weight,
        level3_inverse,
    )
    return tuple(value[None] for value in outputs)


def solution(mesh):
    both = ("sub", "loc")
    cube, flat = P(both, None, None), P(both, None)
    group, group_cube = P("sub", None), P("sub", None, None)
    placed = (cube, cube, cube, flat, cube, cube, flat, group, group_cube, group, group, P())
    return jax.shard_map(
        functools.partial(on_device, mesh),
        mesh=mesh,
        in_specs=placed,
        out_specs=(cube, cube),
        check_vma=False,
    )
```
